128 devices in a mesh: bucket: 64 (over y, x, z_lo, core), grp: 2 (over z_hi).
Axes of the slice: x: 4, y: 4, z: 4 (z_hi: 2, z_lo: 2; z = z_hi * 2 + z_lo), core: 2. Of those that a mesh axis runs over, the one named last changes fastest.
Arguments:
- entities: float32 [131072, 128], P('bucket'), may hold values from -1.8 to 1.8
- ent_accum: float32 [131072], P('bucket'), may hold values from 0.05 to 4
- relations: float32 [128, 128, 128], replicated, may hold values from -0.5 to 0.5
- rel_accum: float32 [128, 128], replicated, may hold values from 1 to 64
- left_index: int32 [64, 2, 16, 1024], P('bucket', 'grp'), may hold values from 0 to 2047
- right_index: int32 [64, 2, 16, 1024], P('bucket', 'grp'), may hold values from 0 to 2047
- batch_rel: int32 [64, 2, 16], P('bucket', 'grp'), may hold values from 0 to 127
- neg_index: int32 [64, 2, 16, 1024], P('bucket', 'grp'), may hold values from 0 to 2047
- batch_count: int32 [64, 2], P('bucket', 'grp'), may hold values from 1 to 16, as said below
- shift: int32 [1], replicated, may hold values from 0 to 1048575
Outputs:
- new_entities: float32 [131072, 128], P('bucket')
- new_ent_accum: float32 [131072], P('bucket')
- new_relations: float32 [128, 128, 128], replicated
- new_rel_accum: float32 [128, 128], replicated
The draws below stay inside these ranges and needn't reach their ends.
Inputs may be any that keep to these rules, and one draw needn't show every extreme that they name: `batch_count`: every draw has an edge list with exactly 16 valid batches.
All inputs are finite; a program needn't handle non-finite values.
Results may differ from the reference program's by a relative error of at most 0.0024.
Values may be sent and summed in bfloat16 or wider, within the bound.
A program may use at most 128 MiB of HBM per device.

```python
import math
import jax
import jax.numpy as jnp
from jax import lax

D = 128
R = 128
ENT = 2048
BATCH = 1024
NEG = 1024
MAXB = 16
ENTITIES = 131072
N_BUCKET = 64
N_GRP = 2


def draw_batch_count(key, part):
    key = jax.random.fold_in(key, 11)
    first, second = jax.random.split(key)
    counts = jax.random.randint(first, (N_BUCKET * N_GRP,), 1, MAXB + 1)
    spot = jax.random.randint(second, (), 0, N_BUCKET * N_GRP)
    counts = jnp.where(jnp.arange(N_BUCKET * N_GRP) == spot, MAXB, counts)
    return counts.reshape(N_BUCKET, N_GRP).astype(jnp.int32)


def with_ends(drawn, stream_key, smallest, largest):
    dims = drawn.shape
    index_at = [jax.random.randint(jax.random.fold_in(stream_key, axis), (), 0, dims[axis]) for axis in range(len(dims))]
    drawn = drawn.at[tuple(index_at)].set(smallest)
    longest = dims.index(max(dims))
    index_at[longest] = (index_at[longest] + 1) % dims[longest]
    return drawn.at[tuple(index_at)].set(largest)


def block_levels(stream_key, extent, shards, low, high):
    loudness, own = 1.0, jax.random.fold_in(stream_key, 6)
    for dim, blocks in shards:
        heights = jnp.exp(jax.random.uniform(jax.random.fold_in(own, dim), (blocks,), jnp.float32, low / len(shards), high / len(shards)))
        loudness = loudness * jnp.repeat(heights, extent[dim] // blocks).reshape([-1 if axis == dim else 1 for axis in range(len(extent))])
    return loudness


def bell_draw(own_key, extent, deviation, reach, cuts=(), held_as=jnp.bfloat16):
    result = jax.random.normal(own_key, extent, jnp.float32) * deviation
    if len(cuts) > 0:
        result = block_levels(own_key, extent, cuts, -0.22, 0.18) * result
    return jnp.clip(result, min=-reach, max=reach).astype(held_as)


def setup_inputs(seed: int = 0) -> dict:
    streams_of = jax.random.split(jax.random.key(seed), 11)
    return {
        "entities": bell_draw(streams_of[0], (ENTITIES, D), 0.3, 1.8, ((0, 64),), jnp.float32),
        "ent_accum": jnp.clip(jnp.exp(math.log(4.0) - 4.3820266 * jax.random.uniform(streams_of[1], (ENTITIES,), jnp.float32) ** block_levels(streams_of[1], (ENTITIES,), ((0, 64),), -0.2, 0.2)), 0.05, 4.0),
        "relations": bell_draw(streams_of[2], (R, D, D), D ** -0.5, 0.5, (), jnp.float32),
        "rel_accum": jnp.clip(jnp.exp(jax.random.uniform(streams_of[3], (R, D), jnp.float32, math.log(1.0), math.log(64.0))), 1.0, 64.0),
        "left_index": with_ends(jax.random.randint(streams_of[4], (N_BUCKET, N_GRP, MAXB, BATCH), 0, ENT), jax.random.fold_in(streams_of[4], 1), 0, ENT - 1).astype(jnp.int32),
        "right_index": with_ends(jax.random.randint(streams_of[5], (N_BUCKET, N_GRP, MAXB, BATCH), 0, ENT), jax.random.fold_in(streams_of[5], 1), 0, ENT - 1).astype(jnp.int32),
        "batch_rel": with_ends(jax.random.randint(streams_of[6], (N_BUCKET, N_GRP, MAXB), 0, R), jax.random.fold_in(streams_of[6], 1), 0, R - 1).astype(jnp.int32),
        "neg_index": with_ends(jax.random.randint(streams_of[7], (N_BUCKET, N_GRP, MAXB, NEG), 0, ENT), jax.random.fold_in(streams_of[7], 1), 0, ENT - 1).astype(jnp.int32),
        "batch_count": draw_batch_count(jax.random.fold_in(streams_of[10], 71), 0),
        "shift": jax.random.randint(streams_of[9], (1,), 0, 1048576).astype(jnp.int32),
    }


RATE = 0.1

def contract(left, right, left_dim, right_dim):
    return lax.dot_general(left, right, (((left_dim,), (right_dim,)), ((), ())), preferred_element_type=jnp.float32)

def batch_terms(left_part, right_part, rel_bf, left_ids, right_ids, neg_ids, rel_id):
    left_rows = jnp.take(left_part, left_ids, axis=0)
    operator = lax.dynamic_index_in_dim(rel_bf, rel_id, 0, keepdims=False)
    query = contract(left_rows, operator, 1, 0)
    query_bf = query.astype(jnp.bfloat16)
    right_rows = jnp.take(right_part, right_ids, axis=0)
    negatives = jnp.take(right_part, neg_ids, axis=0)
    positive = lax.optimization_barrier(jnp.sum(query * right_rows.astype(jnp.float32), axis=1))
    negative = contract(query_bf, negatives, 1, 1)
    pos_grad = -jax.nn.sigmoid(-positive)
    neg_grad = (jax.nn.sigmoid(negative) / negatives.shape[0]).astype(jnp.bfloat16)
    query_grad = pos_grad[:, None] * right_rows.astype(jnp.float32) + contract(neg_grad, negatives, 1, 0)
    query_grad_bf = query_grad.astype(jnp.bfloat16)
    left_grad = contract(query_grad_bf, operator, 1, 1)
    operator_grad = contract(left_rows, query_grad_bf, 0, 0)
    right_grad = pos_grad[:, None] * query
    negative_grad = contract(neg_grad, query_bf, 0, 0)
    return (left_grad, operator_grad, right_grad, negative_grad)

def adagrad_rows(param, accum, grad):
    new_accum = accum + lax.optimization_barrier(jnp.mean(grad * grad, axis=-1))
    return (param - RATE * grad / jnp.sqrt(new_accum)[..., None], new_accum)

def reference(entities, ent_accum, relations, rel_accum, left_index, right_index, batch_rel, neg_index, batch_count, shift):
    ent_bf = entities.astype(jnp.bfloat16)
    rel_bf = relations.astype(jnp.bfloat16)
    offset = (1 + shift[0].astype(jnp.int32) % (N_BUCKET - 1)).astype(jnp.int32)

    def device_step(device, carry):
        entity_grads, operator_sum = carry
        bucket = (device // N_GRP).astype(jnp.int32)
        member = (device % N_GRP).astype(jnp.int32)
        partner = ((bucket + offset) % N_BUCKET).astype(jnp.int32)
        left_start = (bucket * ENT).astype(jnp.int32)
        right_start = (partner * ENT).astype(jnp.int32)
        left_part = lax.dynamic_slice_in_dim(ent_bf, left_start, ENT, 0)
        right_part = lax.dynamic_slice_in_dim(ent_bf, right_start, ENT, 0)
        lefts = left_index[bucket, member]
        rights = right_index[bucket, member]
        negs = neg_index[bucket, member]
        rels = batch_rel[bucket, member]

        def one_batch(slot, inner):
            left_sum, right_sum, op_sum = inner
            left_ids = lefts[slot]
            right_ids = rights[slot]
            neg_ids = negs[slot]
            rel_id = rels[slot]
            left_grad, operator_grad, right_grad, negative_grad = batch_terms(left_part, right_part, rel_bf, left_ids, right_ids, neg_ids, rel_id)
            left_sum = left_sum.at[left_ids].add(left_grad)
            right_sum = right_sum.at[right_ids].add(right_grad).at[neg_ids].add(negative_grad)
            op_sum = op_sum.at[rel_id].add(operator_grad)
            return (left_sum, right_sum, op_sum)
        zeros = jnp.zeros((ENT, D), jnp.float32)
        left_sum, right_sum, operator_sum = lax.fori_loop(jnp.int32(0), batch_count[bucket, member].astype(jnp.int32), one_batch, (zeros, zeros, operator_sum))
        current = lax.dynamic_slice_in_dim(entity_grads, left_start, ENT, 0)
        entity_grads = lax.dynamic_update_slice_in_dim(entity_grads, current + left_sum, left_start, 0)
        current = lax.dynamic_slice_in_dim(entity_grads, right_start, ENT, 0)
        entity_grads = lax.dynamic_update_slice_in_dim(entity_grads, current + right_sum, right_start, 0)
        return (entity_grads, operator_sum)
    start = (jnp.zeros((N_BUCKET * ENT, D), jnp.float32), jnp.zeros((R, D, D), jnp.float32))
    entity_grads, operator_sum = lax.fori_loop(jnp.int32(0), jnp.int32(N_BUCKET * N_GRP), device_step, start)
    new_entities, new_ent_accum = adagrad_rows(entities, ent_accum, entity_grads)
    new_relations, new_rel_accum = adagrad_rows(relations, rel_accum, operator_sum)
    return (new_entities, new_ent_accum, new_relations, new_rel_accum)
```

```python
import jax
import jax.numpy as jnp
from jax import lax
from jax.experimental import pallas as pl
from jax.experimental.pallas import tpu as pltpu
from jax.sharding import PartitionSpec as P

RATE = 0.1
bf=jnp.bfloat16; f32=jnp.float32
def dg(a,b,ca,cb): return lax.dot_general(a,b,(((ca,),(cb,)),((),())),preferred_element_type=f32)
ACC=2
CH=512
JB=256
def train_kernel(count_ref, rel_ref, lid_ref, rid_ref, lp_ref, rp_ref, rrow_ref, nrow_ref, relations_ref,
                 left_out, right_out, op_out,
                 ops, xs, ys, dxs, rpf, drt, sems, *accs):
    E=lp_ref.shape[0]; B=nrow_ref.shape[-1]; NBAT=rel_ref.shape[0]
    NC=B//CH
    count=count_ref[0]
    def opcopy(k):
        return pltpu.make_async_copy(relations_ref.at[rel_ref[k]], ops.at[k], sems.at[k])
    for k in range(NBAT): opcopy(k).start()
    rpf[...]=rp_ref[...].astype(f32)
    for a in accs: a[...]=jnp.zeros_like(a)
    drt[...]=jnp.zeros_like(drt)
    for d in dxs: d[...]=jnp.zeros_like(d)
    op_out[...]=jnp.zeros_like(op_out)
    def gather(base,slot,u0,n):
        for u in range(u0,u0+n):
            xs[slot][u:u+1,:]=lp_ref[pl.ds(lid_ref[base+u],1),:]
            ys[slot][u:u+1,:]=rpf[pl.ds(rid_ref[base+u],1),:]
    def scatter(base,slot,u0,n):
        for u in range(u0,u0+n):
            acc=accs[u%len(accs)]
            acc[pl.ds(lid_ref[base+u],1),:]+=dxs[slot][u:u+1,:]
    gather(0,0,0,CH)
    for k in range(NBAT): opcopy(k).wait()
    lane=lax.broadcasted_iota(jnp.int32,(CH,128),1)
    NJ=E//JB
    def batch(k,_):
        nxt=jnp.minimum(k+1,NBAT-1); prev=jnp.maximum(k-1,0)
        op=ops[k].astype(bf)
        nr=nrow_ref[k]
        lo=(lax.broadcasted_iota(jnp.int32,(128,B),0)==(nr&127)).astype(f32).astype(bf)
        hi=(lax.broadcasted_iota(jnp.int32,(E//128,B),0)==(nr>>7)).astype(f32).astype(bf)
        w=dg(hi,lo,1,1)*(0.5/B)
        rel=rel_ref[k]
        for c in range(NC):
            slot=c%2; other=1-slot
            gbase=k*B+(c+1)*CH if c+1<NC else nxt*B
            sbase=k*B+(c-1)*CH if c>0 else prev*B+(NC-1)*CH
            xb=xs[slot][...].astype(bf)
            y=ys[slot][...]
            q=dg(xb,op,1,0)
            qb=q.astype(bf); qh=(q*0.5).astype(bf)
            qt=q.T.astype(bf)
            pos=jnp.sum(q*y,axis=1,keepdims=True)
            gp=-jax.nn.sigmoid(-pos)
            gpb=jnp.broadcast_to(gp,(CH,128))
            rb=jnp.concatenate([jnp.broadcast_to(rrow_ref[k,c*(CH//128)+m:c*(CH//128)+m+1,:],(128,128)).T for m in range(CH//128)],axis=0)
            dq=gpb*y
            per=CH//NJ
            for j in range(NJ):
                r=rp_ref[j*JB:(j+1)*JB,:]
                s=dg(qh,r,1,1)
                gn=[];g2=[]
                for h in range(JB//128):
                    jj=j*(JB//128)+h
                    th=jnp.tanh(s[:,h*128:(h+1)*128])
                    wj=w[jj:jj+1,:]
                    g=th*wj+wj
                    gn.append(g.astype(bf))
                    g2.append((g+jnp.where(rb==lane+jj*128,gpb,0.0)).astype(bf))
                gn=jnp.concatenate(gn,axis=1);g2=jnp.concatenate(g2,axis=1)
                dq=dq+dg(gn,r,1,0)
                drt[:,j*JB:(j+1)*JB]+=dg(qt,g2,1,0)
                gather(gbase,other,j*per,per)
                scatter(sbase,other,j*per,per)
            dqb=dq.astype(bf)
            dxs[slot][...]=dg(dqb,op,1,1)
            op_out[pl.ds(rel,1)]+=dg(xb,dqb,0,0)[None]
        return 0
    lax.fori_loop(0,count,batch,0)
    scatter((count-1)*B+(NC-1)*CH,(NC-1)%2,0,CH)
    @pl.loop(0,E//128)
    def _(t):
        sl=pl.ds(pl.multiple_of(t*128,128),128)
        tot=accs[0][sl,:]
        for a in accs[1:]: tot=tot+a[sl,:]
        left_out[sl,:]=tot
        right_out[sl,:]=drt[:,sl].T.astype(right_out.dtype)
def train(count,rels,lids,rids,negs,entities,right_bf,relations):
    E=entities.shape[0]; NBAT,B=lids.shape; R=relations.shape[0]
    V=pltpu.VMEM; S=pltpu.SMEM
    sp=lambda m: pl.BlockSpec(memory_space=m)
    def body(*refs):
        ins=refs[:12]; ops,x0,x1,y0,y1,d0,d1,rpf,drt,sems=refs[12:22]
        train_kernel(*ins,ops,(x0,x1),(y0,y1),(d0,d1),rpf,drt,sems,*refs[22:])
    return pl.pallas_call(body,name="train",
      in_specs=[sp(S),sp(S),sp(S),sp(S),sp(V),sp(V),sp(V),sp(V),sp(pl.ANY)],
      out_specs=[sp(V),sp(V),sp(V)],
      out_shape=[jax.ShapeDtypeStruct((E,128),f32),jax.ShapeDtypeStruct((E,128),bf),jax.ShapeDtypeStruct((R,128,128),f32)],
      scratch_shapes=[V((NBAT,128,128),f32)]+[V((CH,128),f32)]*6+[V((E,128),f32),V((128,E),f32),pltpu.SemaphoreType.DMA((NBAT,))]+[V((E,128),f32)]*ACC,
      compiler_params=pltpu.CompilerParams(vmem_limit_bytes=56<<20),
    )(count,rels,lids.reshape(-1),rids.reshape(-1),entities,right_bf,rids.reshape(NBAT,B//128,128),negs.reshape(NBAT,1,B),relations)


def adagrad_rows(param, accum, grad):
    new_accum = accum + jnp.mean(grad * grad, axis=-1)
    return (param - RATE * grad / jnp.sqrt(new_accum)[..., None], new_accum)


def shifted(value, steps):
    count = lax.axis_size("bucket")

    def one(d):
        return lambda v: lax.ppermute(v, "bucket", [(s, (s + d) % count) for s in range(count)])

    return lax.switch(steps - 1, [one(d) for d in range(1, count)], value)


def local(entities, ent_accum, relations, rel_accum, left_index, right_index, batch_rel, neg_index, batch_count, shift):
    bucket_size = lax.axis_size("bucket")
    backward = 1 + shift[0] % (bucket_size - 1)
    right_part = shifted(entities.astype(bf), bucket_size - backward)
    left_sum, right_sum, op_sum = train(batch_count[0], batch_rel[0, 0], left_index[0, 0], right_index[0, 0], neg_index[0, 0], entities, right_part, relations)
    operator_total = lax.psum(op_sum, ("bucket", "grp"))
    own = (left_sum + shifted(right_sum, backward).astype(f32)).astype(bf)
    other = lax.ppermute(own, "grp", [(0, 1), (1, 0)])
    new_entities, new_ent_accum = adagrad_rows(entities, ent_accum, own.astype(f32) + other.astype(f32))
    new_relations, new_rel_accum = adagrad_rows(relations, rel_accum, operator_total)
    return (new_entities, new_ent_accum, new_relations, new_rel_accum)


def solution(mesh):
    placed = (
        P("bucket", None),
        P("bucket"),
        P(),
        P(),
        P("bucket", "grp", None, None),
        P("bucket", "grp", None, None),
        P("bucket", "grp", None),
        P("bucket", "grp", None, None),
        P("bucket", "grp"),
        P(),
    )
    return jax.shard_map(
        local,
        mesh=mesh,
        in_specs=placed,
        out_specs=(P("bucket", None), P("bucket"), P(), P()),
        check_vma=False,
    )
```

```python
import jax
import jax.numpy as jnp
from jax import lax
from jax.experimental import pallas as pl
from jax.experimental.pallas import tpu as pltpu
from jax.sharding import PartitionSpec as P

RATE = 0.1
bf=jnp.bfloat16; f32=jnp.float32
def dg(a,b,ca,cb): return lax.dot_general(a,b,(((ca,),(cb,)),((),())),preferred_element_type=f32)
ACC=2
CH=1024
JB=256
def train_kernel(count_ref, rel_ref, lid_ref, rid_ref, lp_ref, rp_ref, rrow_ref, nrow_ref, relations_ref,
                 left_out, right_out, op_out,
                 ops, xs, ys, dxs, rpf, drt, sems, *accs):
    E=lp_ref.shape[0]; B=nrow_ref.shape[-1]; NBAT=rel_ref.shape[0]
    NC=B//CH
    count=count_ref[0]
    def opcopy(k):
        return pltpu.make_async_copy(relations_ref.at[rel_ref[k]], ops.at[k], sems.at[k])
    for k in range(NBAT): opcopy(k).start()
    rpf[...]=rp_ref[...].astype(f32)
    for a in accs: a[...]=jnp.zeros_like(a)
    drt[...]=jnp.zeros_like(drt)
    for d in dxs: d[...]=jnp.zeros_like(d)
    op_out[...]=jnp.zeros_like(op_out)
    def gather(base,slot,u0,n):
        for u in range(u0,u0+n):
            xs[slot][u:u+1,:]=lp_ref[pl.ds(lid_ref[base+u],1),:]
            ys[slot][u:u+1,:]=rpf[pl.ds(rid_ref[base+u],1),:]
    def scatter(base,slot,u0,n):
        for u in range(u0,u0+n):
            acc=accs[u%len(accs)]
            acc[pl.ds(lid_ref[base+u],1),:]+=dxs[slot][u:u+1,:]
    gather(0,0,0,CH)
    for k in range(NBAT): opcopy(k).wait()
    lane=lax.broadcasted_iota(jnp.int32,(CH,128),1)
    NJ=E//JB
    def batch(k,_):
        nxt=jnp.minimum(k+1,NBAT-1); prev=jnp.maximum(k-1,0)
        op=ops[k].astype(bf)
        nr=nrow_ref[k]
        lo=(lax.broadcasted_iota(jnp.int32,(128,B),0)==(nr&127)).astype(f32).astype(bf)
        hi=(lax.broadcasted_iota(jnp.int32,(E//128,B),0)==(nr>>7)).astype(f32).astype(bf)
        w=(dg(hi,lo,1,1)*(0.5/B)).astype(bf)
        rel=rel_ref[k]
        for c in range(NC):
            slot=other=0
            gbase=k*B+(c+1)*CH if c+1<NC else nxt*B
            sbase=k*B+(c-1)*CH if c>0 else prev*B+(NC-1)*CH
            xb=xs[slot][...].astype(bf)
            y=ys[slot][...]
            q=dg(xb,op,1,0)
            qb=q.astype(bf); qh=(q*0.5).astype(bf)
            qt=q.T.astype(bf)
            pos=jnp.sum(q*y,axis=1,keepdims=True)
            gp=-jax.nn.sigmoid(-pos)
            gpb=jnp.broadcast_to(gp,(CH,128))
            rb=jnp.concatenate([jnp.broadcast_to(rrow_ref[k,c*(CH//128)+m:c*(CH//128)+m+1,:],(128,128)).T for m in range(CH//128)],axis=0)
            dq=gpb*y
            hib=(rb>>7).astype(f32).astype(bf)
            hot=jnp.where((rb&127)==lane,gpb,0.0).astype(bf)
            per=CH//NJ
            for j in range(NJ):
                r=rp_ref[j*JB:(j+1)*JB,:]
                s=dg(qh,r,1,1)
                sb=s.astype(bf)
                gn=[];g2=[]
                for h in range(JB//128):
                    jj=j*(JB//128)+h
                    th=jnp.tanh(sb[:,h*128:(h+1)*128])
                    wj=w[jj:jj+1,:]
                    g=th*wj+wj
                    gn.append(g)
                    g2.append(g+jnp.where(hib==bf(jj),hot,bf(0)))
                gn=jnp.concatenate(gn,axis=1);g2=jnp.concatenate(g2,axis=1)
                dq=dq+dg(gn,r,1,0)
                drt[:,j*JB:(j+1)*JB]+=dg(qt,g2,1,0)
                gather(gbase,other,j*per,per)
                scatter(sbase,other,j*per,per)
            dqb=dq.astype(bf)
            dxs[slot][...]=dg(dqb,op,1,1)
            op_out[pl.ds(rel,1)]+=dg(xb,dqb,0,0)[None]
        return 0
    lax.fori_loop(0,count,batch,0)
    scatter((count-1)*B,0,0,CH)
    @pl.loop(0,E//128)
    def _(t):
        sl=pl.ds(pl.multiple_of(t*128,128),128)
        tot=accs[0][sl,:]
        for a in accs[1:]: tot=tot+a[sl,:]
        left_out[sl,:]=tot
        right_out[sl,:]=drt[:,sl].T.astype(right_out.dtype)
def train(count,rels,lids,rids,negs,entities,right_bf,relations):
    E=entities.shape[0]; NBAT,B=lids.shape; R=relations.shape[0]
    V=pltpu.VMEM; S=pltpu.SMEM
    sp=lambda m: pl.BlockSpec(memory_space=m)
    def body(*refs):
        ins=refs[:12]; ops,x0,y0,d0,rpf,drt,sems=refs[12:19]
        train_kernel(*ins,ops,(x0,),(y0,),(d0,),rpf,drt,sems,*refs[19:])
    return pl.pallas_call(body,name="train",
      in_specs=[sp(S),sp(S),sp(S),sp(S),sp(V),sp(V),sp(V),sp(V),sp(pl.ANY)],
      out_specs=[sp(V),sp(V),sp(V)],
      out_shape=[jax.ShapeDtypeStruct((E,128),f32),jax.ShapeDtypeStruct((E,128),bf),jax.ShapeDtypeStruct((R,128,128),f32)],
      scratch_shapes=[V((NBAT,128,128),f32)]+[V((CH,128),f32)]*3+[V((E,128),f32),V((128,E),f32),pltpu.SemaphoreType.DMA((NBAT,))]+[V((E,128),f32)]*ACC,
      compiler_params=pltpu.CompilerParams(vmem_limit_bytes=56<<20),
    )(count,rels,lids.reshape(-1),rids.reshape(-1),entities,right_bf,rids.reshape(NBAT,B//128,128),negs.reshape(NBAT,1,B),relations)


MESH = pl.DeviceIdType.MESH
GROUPS = ((0, 48, "zyx"), (48, 48, "yxz"), (96, 32, "xzy"))


def op_sum_kernel(g_ref, out, own, sib, snd, r1a, r1b, r1c, t1a, t1b, t1c, r2a, r2b, r2c, t2a, t2b, t2c, r3a, r3b, r3c,
                  local_sem, a_sem, s1_sem, s2_sem, s3_sem, g1_sem, g2_sem, g3_sem, c_sem):
    r1s, t1s, r2s, t2s, r3s = (r1a, r1b, r1c), (t1a, t1b, t1c), (r2a, r2b, r2c), (t2a, t2b, t2c), (r3a, r3b, r3c)
    b = lax.axis_index("bucket")
    core = b % 2
    me = {"y": b // 16, "x": (b // 4) % 4, "z": lax.axis_index("grp") * 2 + (b // 2) % 2}

    def device(at, c):
        return {"bucket": at["y"] * 16 + at["x"] * 4 + (at["z"] % 2) * 2 + c, "grp": at["z"] // 2}

    def moved(axis, o):
        return dict(me, **{axis: (me[axis] + o) % 4})

    def peer(axis, o):
        return device(moved(axis, o), core)

    sibling = device(me, 1 - core)

    def send(src, dst, sems, at, target):
        return pltpu.make_async_remote_copy(src_ref=src, dst_ref=dst, send_sem=sems.at[(0,) + at], recv_sem=sems.at[(1,) + at],
                                            device_id=target, device_id_type=MESH)

    barrier = pltpu.get_barrier_semaphore()
    pl.semaphore_signal(barrier, inc=1, device_id=sibling, device_id_type=MESH)
    for axis in "yxz":
        for o in (1, 2, 3):
            pl.semaphore_signal(barrier, inc=1, device_id=peer(axis, o), device_id_type=MESH)
    locals_ = []
    order = [(me["y"] + o) % 4 for o in (1, 2, 3, 0)]
    for i, p in enumerate(order):
        c = pltpu.make_async_copy(g_ref.at[core, p], own.at[p], local_sem.at[i])
        c.start()
        locals_.append(c)
    pl.semaphore_wait(barrier, 10)
    across = []
    for i, p in enumerate(order):
        c = send(g_ref.at[1 - core, p], sib.at[p], a_sem, (i,), sibling)
        c.start()
        across.append(c)
    firsts = []
    for i, p in enumerate(order):
        locals_[i].wait()
        across[i].wait_recv()

        @pl.loop(0, 4)
        def _(x):
            total = own[p, x] + sib[p, x]
            own[p, x] = total
            snd[p, x] = total.astype(bf)

        for o in (1, 2, 3):
            rows = pl.ds(0, 48)
            c = send(snd.at[p, :, (me["z"] + o) % 4, rows], r1a.at[o - 1, p], s1_sem, (0, o - 1, i), peer("z", o))
            c.start()
            firsts.append(c)
            rows = pl.ds(96, 32)
            c = send(snd.at[p, (me["x"] + o) % 4, :, rows], r1c.at[o - 1, :, p], s1_sem, (2, o - 1, i), peer("x", o))
            c.start()
            firsts.append(c)
        if i < 3:
            o = i + 1
            c = send(snd.at[p, :, :, pl.ds(48, 48)], r1b.at[o - 1], s1_sem, (1, o - 1, 0), peer("y", o))
            c.start()
            firsts.append(c)
    for c in firsts:
        c.wait_recv()

    @pl.loop(0, 4)
    def _(u):
        for v in range(4):
            for k, (start, n, _) in enumerate(GROUPS):
                rows = pl.ds(start, n)
                part = (own.at[u, v, me["z"], rows], own.at[me["y"], u, v, rows], own.at[v, me["x"], u, rows])[k][...]
                for o in range(3):
                    part = part + r1s[k][o, u, v].astype(f32)
                t1s[k][u, v] = part

    seconds = []
    for k, (start, n, axes) in enumerate(GROUPS):
        for o in (1, 2, 3):
            c = send(t1s[k].at[(me[axes[1]] + o) % 4], r2s[k].at[o - 1], s2_sem, (k, o - 1), peer(axes[1], o))
            c.start()
            seconds.append(c)
    for c in seconds:
        c.wait_recv()
    for k, (start, n, axes) in enumerate(GROUPS):
        t2s[k][...] = t1s[k][me[axes[1]]] + r2s[k][0] + r2s[k][1] + r2s[k][2]
    thirds = []
    for k, (start, n, axes) in enumerate(GROUPS):
        for o in (1, 2, 3):
            c = send(t2s[k].at[(me[axes[2]] + o) % 4], r3s[k].at[o - 1], s3_sem, (k, o - 1), peer(axes[2], o))
            c.start()
            thirds.append(c)
    for c in thirds:
        c.wait_recv()
    gathers = []

    def place(k, free, at):
        start, n, _ = GROUPS[k]
        index = tuple(slice(None) if a in free else at[a] for a in "yxz")
        return out.at[(core,) + index + (pl.ds(start, n),)]

    for k, (start, n, axes) in enumerate(GROUPS):
        total = t2s[k][me[axes[2]]] + r3s[k][0] + r3s[k][1] + r3s[k][2]
        out[core, me["y"], me["x"], me["z"], pl.ds(start, n)] = total.astype(bf)
    for level, sems in ((2, g1_sem), (1, g2_sem), (0, g3_sem)):
        started = []
        for k, (start, n, axes) in enumerate(GROUPS):
            ref = place(k, axes[level + 1:], me)
            for o in (1, 2, 3):
                c = send(ref, ref, sems, (k, o - 1), peer(axes[level], o))
                c.start()
                started.append(c)
            if level == 0:
                c = send(ref, ref, c_sem, (k, 3), sibling)
                c.start()
                gathers.append(c)
        for i, c in enumerate(started):
            c.wait_recv()
            if level == 0:
                k, o = i // 3, i % 3 + 1
                axes = GROUPS[k][2]
                ref = place(k, axes[1:], moved(axes[0], 4 - o))
                f = send(ref, ref, c_sem, (k, o - 1), sibling)
                f.start()
                gathers.append(f)
        gathers.extend([] for _ in ())
        for c in started:
            c.wait_send()
    for c in gathers:
        c.wait_recv()
        c.wait_send()
    for c in across + firsts + seconds + thirds:
        c.wait_send()


def op_total(op_sum):
    V = pltpu.VMEM
    D = pltpu.SemaphoreType.DMA
    ns = [n for _, n, _ in GROUPS]
    shapes = [V((4, 4, 4, 128, 128), f32), V((4, 4, 4, 128, 128), f32), V((4, 4, 4, 128, 128), bf)]
    shapes += [V((3, 4, 4, n, 128), bf) for n in ns] + [V((4, 4, n, 128), f32) for n in ns]
    shapes += [V((3, 4, n, 128), f32) for n in ns] + [V((4, n, 128), f32) for n in ns] + [V((3, n, 128), f32) for n in ns]
    sems = [D((4,)), D((2, 4)), D((2, 3, 3, 4))] + [D((2, 3, 3))] * 5 + [D((2, 3, 4))]
    out = pl.pallas_call(
        op_sum_kernel,
        name="op_total",
        in_specs=[pl.BlockSpec(memory_space=pl.ANY)],
        out_specs=pl.BlockSpec(memory_space=V),
        out_shape=jax.ShapeDtypeStruct((2, 4, 4, 4, 128, 128), bf),
        scratch_shapes=shapes + sems,
        compiler_params=pltpu.CompilerParams(collective_id=0, has_side_effects=True, vmem_limit_bytes=40 << 20),
    )(op_sum.reshape(2, 4, 4, 4, 128, 128))
    return out.reshape(128, 128, 128)


def op_update_kernel(g_ref, p_ref, a_ref, np_ref, na_ref):
    g = g_ref[...].astype(f32)
    acc = a_ref[...] + jnp.mean(g * g, axis=-1)
    na_ref[...] = acc
    np_ref[...] = p_ref[...] - g * (0.1 / jnp.sqrt(acc))[..., None]


def op_update(total, relations, rel_accum):
    n = 8
    cube = pl.BlockSpec((n, 128, 128), lambda i: (i, 0, 0))
    rows = pl.BlockSpec((n, 128), lambda i: (i, 0))
    return pl.pallas_call(op_update_kernel, name="op_update", grid=(128 // n,), in_specs=[cube, cube, rows], out_specs=[cube, rows],
                          out_shape=[jax.ShapeDtypeStruct(relations.shape, f32), jax.ShapeDtypeStruct(rel_accum.shape, f32)],
                          compiler_params=pltpu.CompilerParams(vmem_limit_bytes=32 << 20))(total, relations, rel_accum)


def adagrad_rows(param, accum, grad):
    new_accum = accum + jnp.mean(grad * grad, axis=-1)
    return (param - RATE * grad / jnp.sqrt(new_accum)[..., None], new_accum)


def shifted(value, steps):
    count = lax.axis_size("bucket")

    def one(d):
        return lambda v: lax.ppermute(v, "bucket", [(s, (s + d) % count) for s in range(count)])

    return lax.switch(steps - 1, [one(d) for d in range(1, count)], value)


def local(entities, ent_accum, relations, rel_accum, left_index, right_index, batch_rel, neg_index, batch_count, shift):
    bucket_size = lax.axis_size("bucket")
    backward = 1 + shift[0] % (bucket_size - 1)
    right_part = shifted(entities.astype(bf), bucket_size - backward)
    left_sum, right_sum, op_sum = train(batch_count[0], batch_rel[0, 0], left_index[0, 0], right_index[0, 0], neg_index[0, 0], entities, right_part, relations)
    new_relations, new_rel_accum = op_update(op_total(op_sum), relations, rel_accum)
    own = (left_sum + shifted(right_sum, backward).astype(f32)).astype(bf)
    other = lax.ppermute(own, "grp", [(0, 1), (1, 0)])
    new_entities, new_ent_accum = adagrad_rows(entities, ent_accum, own.astype(f32) + other.astype(f32))
    return (new_entities, new_ent_accum, new_relations, new_rel_accum)


def solution(mesh):
    placed = (
        P("bucket", None),
        P("bucket"),
        P(),
        P(),
        P("bucket", "grp", None, None),
        P("bucket", "grp", None, None),
        P("bucket", "grp", None),
        P("bucket", "grp", None, None),
        P("bucket", "grp"),
        P(),
    )
    return jax.shard_map(
        local,
        mesh=mesh,
        in_specs=placed,
        out_specs=(P("bucket", None), P("bucket"), P(), P()),
        check_vma=False,
    )
```

```python
import jax
import jax.numpy as jnp
from jax import lax
from jax.experimental import pallas as pl
from jax.experimental.pallas import tpu as pltpu
from jax.sharding import PartitionSpec as P

RATE = 0.1
bf=jnp.bfloat16; f32=jnp.float32
def dg(a,b,ca,cb): return lax.dot_general(a,b,(((ca,),(cb,)),((),())),preferred_element_type=f32)
ACC=2
CH=1024
JB=256
def train_kernel(count_ref, rel_ref, lid_ref, rid_ref, lp_ref, rp_ref, rrow_ref, nrow_ref, relations_ref,
                 left_out, right_out, op_out,
                 ops, xs, ys, dxs, rpf, drt, sems, *accs):
    E=lp_ref.shape[0]; B=nrow_ref.shape[-1]; NBAT=rel_ref.shape[0]
    NC=B//CH
    count=count_ref[0]
    def opcopy(k):
        return pltpu.make_async_copy(relations_ref.at[rel_ref[k]], ops.at[k], sems.at[k])
    for k in range(NBAT): opcopy(k).start()
    rpf[...]=rp_ref[...].astype(f32)
    for a in accs: a[...]=jnp.zeros_like(a)
    drt[...]=jnp.zeros_like(drt)
    for d in dxs: d[...]=jnp.zeros_like(d)
    op_out[...]=jnp.zeros_like(op_out)
    def gather(base,slot,u0,n):
        for u in range(u0,u0+n):
            xs[slot][u:u+1,:]=lp_ref[pl.ds(lid_ref[base,u],1),:]
            ys[slot][u:u+1,:]=rpf[pl.ds(rid_ref[base,u],1),:]
    def scatter(base,slot,u0,n):
        for u in range(u0,u0+n):
            acc=accs[u%len(accs)]
            acc[pl.ds(lid_ref[base,u],1),:]+=dxs[slot][u:u+1,:]
    gather(0,0,0,CH)
    for k in range(NBAT): opcopy(k).wait()
    lane=lax.broadcasted_iota(jnp.int32,(CH,128),1)
    NJ=E//JB
    def batch(k,_):
        nxt=jnp.minimum(k+1,NBAT-1); prev=jnp.maximum(k-1,0)
        op=ops[k].astype(bf)
        nr=nrow_ref[pl.ds(k,1),:]
        lo=(lax.broadcasted_iota(jnp.int32,(128,B),0)==(nr&127)).astype(f32).astype(bf)
        hi=(lax.broadcasted_iota(jnp.int32,(E//128,B),0)==(nr>>7)).astype(f32).astype(bf)
        w=(dg(hi,lo,1,1)*(0.5/B)).astype(bf)
        rel=rel_ref[k]
        for c in range(NC):
            slot=other=0
            gbase=nxt
            sbase=prev
            xb=xs[slot][...].astype(bf)
            y=ys[slot][...]
            q=dg(xb,op,1,0)
            qb=q.astype(bf); qh=(q*0.5).astype(bf)
            qt=q.T.astype(bf)
            pos=jnp.sum(q*y,axis=1,keepdims=True)
            gp=-jax.nn.sigmoid(-pos)
            gpb=jnp.broadcast_to(gp,(CH,128))
            rr=rrow_ref[pl.ds(k,1),:]
            rb=jnp.concatenate([jnp.broadcast_to(rr[:,m*128:(m+1)*128],(128,128)).T for m in range(CH//128)],axis=0)
            dq=gpb*y
            hib=(rb>>7).astype(f32).astype(bf)
            hot=jnp.where((rb&127)==lane,gpb,0.0).astype(bf)
            per=CH//NJ
            for j in range(NJ):
                r=rp_ref[j*JB:(j+1)*JB,:]
                s=dg(qh,r,1,1)
                sb=s.astype(bf)
                gn=[];g2=[]
                for h in range(JB//128):
                    jj=j*(JB//128)+h
                    th=jnp.tanh(sb[:,h*128:(h+1)*128])
                    wj=w[jj:jj+1,:]
                    g=th*wj+wj
                    gn.append(g)
                    g2.append(g+jnp.where(hib==bf(jj),hot,bf(0)))
                gn=jnp.concatenate(gn,axis=1);g2=jnp.concatenate(g2,axis=1)
                dq=dq+dg(gn,r,1,0)
                drt[:,j*JB:(j+1)*JB]+=dg(qt,g2,1,0)
                gather(gbase,other,j*per,per)
                scatter(sbase,other,j*per,per)
            dqb=dq.astype(bf)
            dxs[slot][...]=dg(dqb,op,1,1)
            op_out[pl.ds(rel,1)]+=dg(xb,dqb,0,0)[None]
        return 0
    lax.fori_loop(0,count,batch,0)
    scatter(count-1,0,0,CH)
    @pl.loop(0,E//128)
    def _(t):
        sl=pl.ds(pl.multiple_of(t*128,128),128)
        tot=accs[0][sl,:]
        for a in accs[1:]: tot=tot+a[sl,:]
        left_out[sl,:]=tot
        right_out[sl,:]=drt[:,sl].T.astype(right_out.dtype)
def train(count,rels,lids,rids,negs,entities,right_bf,relations):
    E=entities.shape[0]; NBAT,B=lids.shape; R=relations.shape[0]
    V=pltpu.VMEM; S=pltpu.SMEM
    sp=lambda m: pl.BlockSpec(memory_space=m)
    def body(*refs):
        ins=refs[:12]; ops,x0,y0,d0,rpf,drt,sems=refs[12:19]
        train_kernel(*ins,ops,(x0,),(y0,),(d0,),rpf,drt,sems,*refs[19:])
    return pl.pallas_call(body,name="train",
      in_specs=[sp(S),sp(S),sp(S),sp(S),sp(V),sp(V),sp(V),sp(V),sp(pl.ANY)],
      out_specs=[sp(V),sp(V),sp(V)],
      out_shape=[jax.ShapeDtypeStruct((E,128),f32),jax.ShapeDtypeStruct((E,128),bf),jax.ShapeDtypeStruct((R,128,128),f32)],
      scratch_shapes=[V((NBAT,128,128),f32)]+[V((CH,128),f32)]*3+[V((E,128),f32),V((128,E),f32),pltpu.SemaphoreType.DMA((NBAT,))]+[V((E,128),f32)]*ACC,
      compiler_params=pltpu.CompilerParams(vmem_limit_bytes=56<<20),
    )(count,rels,lids,rids,entities,right_bf,rids,negs,relations)


MESH = pl.DeviceIdType.MESH
GROUPS = ((0, 48, "zyx"), (48, 48, "yxz"), (96, 32, "xzy"))


def op_sum_kernel(g_ref, e_ref, out, e_out, own, sib, snd, r1a, r1b, r1c, t1a, t1b, t1c, r2a, r2b, r2c, t2a, t2b, t2c, r3a, r3b, r3c,
                  local_sem, a_sem, s1_sem, s2_sem, s3_sem, g1_sem, g2_sem, g3_sem, c_sem, e_sem):
    r1s, t1s, r2s, t2s, r3s = (r1a, r1b, r1c), (t1a, t1b, t1c), (r2a, r2b, r2c), (t2a, t2b, t2c), (r3a, r3b, r3c)
    b = lax.axis_index("bucket")
    core = b % 2
    me = {"y": b // 16, "x": (b // 4) % 4, "z": lax.axis_index("grp") * 2 + (b // 2) % 2}

    def device(at, c):
        return {"bucket": at["y"] * 16 + at["x"] * 4 + (at["z"] % 2) * 2 + c, "grp": at["z"] // 2}

    def moved(axis, o):
        return dict(me, **{axis: (me[axis] + o) % 4})

    def peer(axis, o):
        return device(moved(axis, o), core)

    sibling = device(me, 1 - core)

    def send(src, dst, sems, at, target):
        return pltpu.make_async_remote_copy(src_ref=src, dst_ref=dst, send_sem=sems.at[(0,) + at], recv_sem=sems.at[(1,) + at],
                                            device_id=target, device_id_type=MESH)

    barrier = pltpu.get_barrier_semaphore()
    pl.semaphore_signal(barrier, inc=1, device_id=sibling, device_id_type=MESH)
    for axis in "yxz":
        for o in (1, 2, 3):
            pl.semaphore_signal(barrier, inc=1, device_id=peer(axis, o), device_id_type=MESH)
    locals_ = []
    order = [(me["y"] + o) % 4 for o in (1, 2, 3, 0)]
    for i, p in enumerate(order):
        c = pltpu.make_async_copy(g_ref.at[core, p], own.at[p], local_sem.at[i])
        c.start()
        locals_.append(c)
    pl.semaphore_wait(barrier, 10)
    exchange = send(e_ref, e_out, e_sem, (0,), peer("z", 2))
    exchange.start()
    across = []
    for i, p in enumerate(order):
        c = send(g_ref.at[1 - core, p], sib.at[p], a_sem, (i,), sibling)
        c.start()
        across.append(c)
    firsts = []
    for i, p in enumerate(order):
        locals_[i].wait()
        across[i].wait_recv()

        @pl.loop(0, 4)
        def _(x):
            total = own[p, x] + sib[p, x]
            own[p, x] = total
            snd[p, x] = total.astype(bf)

        for o in (1, 2, 3):
            rows = pl.ds(0, 48)
            c = send(snd.at[p, :, (me["z"] + o) % 4, rows], r1a.at[o - 1, p], s1_sem, (0, o - 1, i), peer("z", o))
            c.start()
            firsts.append((0, c))
            rows = pl.ds(96, 32)
            c = send(snd.at[p, (me["x"] + o) % 4, :, rows], r1c.at[o - 1, :, p], s1_sem, (2, o - 1, i), peer("x", o))
            c.start()
            firsts.append((2, c))
        if i < 3:
            o = i + 1
            c = send(snd.at[p, :, :, pl.ds(48, 48)], r1b.at[o - 1], s1_sem, (1, o - 1, 0), peer("y", o))
            c.start()
            firsts.append((1, c))
    seconds, thirds, gathers = [], [], {}
    for k, (start, n, axes) in enumerate(GROUPS):
        rows = pl.ds(start, n)
        for g, c in firsts:
            if g == k:
                c.wait_recv()

        @pl.loop(0, 4)
        def _(u):
            for v in range(4):
                part = (own.at[u, v, me["z"], rows], own.at[me["y"], u, v, rows], own.at[v, me["x"], u, rows])[k][...]
                for o in range(3):
                    part = part + r1s[k][o, u, v].astype(f32)
                t1s[k][u, v] = part

        for o in (1, 2, 3):
            c = send(t1s[k].at[(me[axes[1]] + o) % 4], r2s[k].at[o - 1], s2_sem, (k, o - 1), peer(axes[1], o))
            c.start()
            seconds.append(c)
    for k, (start, n, axes) in enumerate(GROUPS):
        for c in seconds[3 * k:3 * k + 3]:
            c.wait_recv()
        t2s[k][...] = t1s[k][me[axes[1]]] + r2s[k][0] + r2s[k][1] + r2s[k][2]
        for o in (1, 2, 3):
            c = send(t2s[k].at[(me[axes[2]] + o) % 4], r3s[k].at[o - 1], s3_sem, (k, o - 1), peer(axes[2], o))
            c.start()
            thirds.append(c)

    def place(k, free, at):
        start, n, _ = GROUPS[k]
        index = tuple(slice(None) if a in free else at[a] for a in "yxz")
        return out.at[(core,) + index + (pl.ds(start, n),)]

    def spread(k, level, sems):
        axes = GROUPS[k][2]
        ref = place(k, axes[level + 1:], me)
        gathers[level, k] = [send(ref, ref, sems, (k, o - 1), peer(axes[level], o)) for o in (1, 2, 3)]
        for c in gathers[level, k]:
            c.start()

    for k, (start, n, axes) in enumerate(GROUPS):
        for c in thirds[3 * k:3 * k + 3]:
            c.wait_recv()
        total = t2s[k][me[axes[2]]] + r3s[k][0] + r3s[k][1] + r3s[k][2]
        out[core, me["y"], me["x"], me["z"], pl.ds(start, n)] = total.astype(bf)
        spread(k, 2, g1_sem)
    for k in range(3):
        for c in gathers[2, k]:
            c.wait_recv()
        spread(k, 1, g2_sem)
    kept = []

    def keep(k, ref, i):
        c = send(ref, ref, c_sem, (k, i), sibling)
        c.start()
        kept.append(c)

    for k in range(3):
        for c in gathers[1, k]:
            c.wait_recv()
        spread(k, 0, g3_sem)
        keep(k, place(k, GROUPS[k][2][1:], me), 3)
    for k in range(3):
        axes = GROUPS[k][2]
        for o in (1, 3, 2):
            gathers[0, k][o - 1].wait_recv()
            keep(k, place(k, axes[1:], moved(axes[0], 4 - o)), o - 1)
    for c in kept:
        c.wait_recv()
    for c in across + [c for _, c in firsts] + seconds + thirds + sum(gathers.values(), []) + kept:
        c.wait_send()
    exchange.wait()


def op_total(op_sum, rows):
    V = pltpu.VMEM
    D = pltpu.SemaphoreType.DMA
    ns = [n for _, n, _ in GROUPS]
    shapes = [V((4, 4, 4, 128, 128), f32), V((4, 4, 4, 128, 128), f32), V((4, 4, 4, 128, 128), bf)]
    shapes += [V((3, 4, 4, n, 128), bf) for n in ns] + [V((4, 4, n, 128), f32) for n in ns]
    shapes += [V((3, 4, n, 128), f32) for n in ns] + [V((4, n, 128), f32) for n in ns] + [V((3, n, 128), f32) for n in ns]
    sems = [D((4,)), D((2, 4)), D((2, 3, 3, 4))] + [D((2, 3, 3))] * 5 + [D((2, 3, 4)), D((2, 1))]
    out, other = pl.pallas_call(
        op_sum_kernel,
        name="op_total",
        in_specs=[pl.BlockSpec(memory_space=pl.ANY), pl.BlockSpec(memory_space=V)],
        out_specs=[pl.BlockSpec(memory_space=V)] * 2,
        out_shape=[jax.ShapeDtypeStruct((2, 4, 4, 4, 128, 128), bf), jax.ShapeDtypeStruct(rows.shape, bf)],
        scratch_shapes=shapes + sems,
        compiler_params=pltpu.CompilerParams(collective_id=0, has_side_effects=True, vmem_limit_bytes=58 << 20),
    )(op_sum.reshape(2, 4, 4, 4, 128, 128), rows)
    return out.reshape(128, 128, 128), other


def op_update_kernel(g_ref, p_ref, a_ref, np_ref, na_ref):
    g = g_ref[...].astype(f32)
    acc = a_ref[...] + jnp.mean(g * g, axis=-1)
    na_ref[...] = acc
    np_ref[...] = p_ref[...] - g * (0.1 / jnp.sqrt(acc))[..., None]


def op_update(total, relations, rel_accum):
    n = 32
    cube = pl.BlockSpec((n, 128, 128), lambda i: (i, 0, 0))
    rows = pl.BlockSpec((n, 128), lambda i: (i, 0))
    return pl.pallas_call(op_update_kernel, name="op_update", grid=(128 // n,), in_specs=[cube, cube, rows], out_specs=[cube, rows],
                          out_shape=[jax.ShapeDtypeStruct(relations.shape, f32), jax.ShapeDtypeStruct(rel_accum.shape, f32)],
                          compiler_params=pltpu.CompilerParams(vmem_limit_bytes=58 << 20))(total, relations, rel_accum)


def adagrad_rows(param, accum, grad):
    new_accum = accum + jnp.mean(grad * grad, axis=-1)
    return (param - RATE * grad / jnp.sqrt(new_accum)[..., None], new_accum)


def shifted(value, steps):
    count = lax.axis_size("bucket")

    def one(d):
        return lambda v: lax.ppermute(v, "bucket", [(s, (s + d) % count) for s in range(count)])

    return lax.switch(steps - 1, [one(d) for d in range(1, count)], value)


def local(entities, ent_accum, relations, rel_accum, left_index, right_index, batch_rel, neg_index, batch_count, shift):
    bucket_size = lax.axis_size("bucket")
    backward = 1 + shift[0] % (bucket_size - 1)
    right_part = shifted(entities.astype(bf), bucket_size - backward)
    left_sum, right_sum, op_sum = train(batch_count[0], batch_rel[0, 0], left_index[0, 0], right_index[0, 0], neg_index[0, 0], entities, right_part, relations)
    own = (left_sum + shifted(right_sum, backward).astype(f32)).astype(bf)
    operator_total, other = op_total(op_sum, own)
    new_relations, new_rel_accum = op_update(operator_total, relations, rel_accum)
    new_entities, new_ent_accum = adagrad_rows(entities, ent_accum, own.astype(f32) + other.astype(f32))
    return (new_entities, new_ent_accum, new_relations, new_rel_accum)


def solution(mesh):
    placed = (
        P("bucket", None),
        P("bucket"),
        P(),
        P(),
        P("bucket", "grp", None, None),
        P("bucket", "grp", None, None),
        P("bucket", "grp", None),
        P("bucket", "grp", None, None),
        P("bucket", "grp"),
        P(),
    )
    return jax.shard_map(
        local,
        mesh=mesh,
        in_specs=placed,
        out_specs=(P("bucket", None), P("bucket"), P(), P()),
        check_vma=False,
    )
```

```python
import jax
import jax.numpy as jnp
from jax import lax
from jax.experimental import pallas as pl
from jax.experimental.pallas import tpu as pltpu
from jax.sharding import PartitionSpec as P

RATE = 0.1
bf=jnp.bfloat16; f32=jnp.float32
def dg(a,b,ca,cb): return lax.dot_general(a,b,(((ca,),(cb,)),((),())),preferred_element_type=f32)
ACC=2
CH=1024
JB=256
def train_kernel(count_ref, rel_ref, lid_any, rid_any, lp_any, rp_any, rrow_any, nrow_any, relations_ref,
                 left_out, right_out, op_any,
                 lid_ref, rid_ref, lp_ref, rp_ref, rrow_ref, nrow_ref, op_out, in_sems, out_sem, id_sems,
                 ops, xs, ys, dxs, rpf, drt, sems, *accs):
    E=lp_ref.shape[0]; B=nrow_ref.shape[-1]; NBAT=rel_ref.shape[0]
    NC=B//CH
    count=count_ref[0]
    def opcopy(k):
        return pltpu.make_async_copy(relations_ref.at[rel_ref[k]], ops.at[k], sems.at[k])
    pairs=((rp_any,rp_ref),(lp_any,lp_ref),(rrow_any,rrow_ref),(nrow_any,nrow_ref))
    incoming=[pltpu.make_async_copy(a,b,in_sems.at[i]) for i,(a,b) in enumerate(pairs)]
    for k in range(NBAT):
        for i,(a,b) in enumerate(((lid_any,lid_ref),(rid_any,rid_ref))):
            incoming.append(pltpu.make_async_copy(a.at[k],b.at[pl.ds(k*B,B)],id_sems.at[i,k]))
    for c in incoming: c.start()
    for k in range(NBAT): opcopy(k).start()
    for a in accs: a[...]=jnp.zeros_like(a)
    drt[...]=jnp.zeros_like(drt)
    for d in dxs: d[...]=jnp.zeros_like(d)
    op_out[...]=jnp.zeros_like(op_out)
    for c in incoming: c.wait()
    rpf[...]=rp_ref[...].astype(f32)
    def gather(base,slot,u0,n):
        for u in range(u0,u0+n):
            xs[slot][u:u+1,:]=lp_ref[pl.ds(lid_ref[base*B+u],1),:]
            ys[slot][u:u+1,:]=rpf[pl.ds(rid_ref[base*B+u],1),:]
    def scatter(base,slot,u0,n):
        for u in range(u0,u0+n):
            acc=accs[u%len(accs)]
            acc[pl.ds(lid_ref[base*B+u],1),:]+=dxs[slot][u:u+1,:]
    gather(0,0,0,CH)
    for k in range(NBAT): opcopy(k).wait()
    lane=lax.broadcasted_iota(jnp.int32,(CH,128),1)
    NJ=E//JB
    def batch(k,_):
        nxt=jnp.minimum(k+1,NBAT-1); prev=jnp.maximum(k-1,0)
        op=ops[k].astype(bf)
        nr=nrow_ref[pl.ds(k,1),:]
        lo=(lax.broadcasted_iota(jnp.int32,(128,B),0)==(nr&127)).astype(f32).astype(bf)
        hi=(lax.broadcasted_iota(jnp.int32,(E//128,B),0)==(nr>>7)).astype(f32).astype(bf)
        w=(dg(hi,lo,1,1)*(0.5/B)).astype(bf)
        rel=rel_ref[k]
        for c in range(NC):
            slot=other=0
            gbase=nxt
            sbase=prev
            xb=xs[slot][...].astype(bf)
            y=ys[slot][...]
            q=dg(xb,op,1,0)
            qb=q.astype(bf); qh=(q*0.5).astype(bf)
            qt=q.T.astype(bf)
            pos=jnp.sum(q*y,axis=1,keepdims=True)
            gp=-jax.nn.sigmoid(-pos)
            gpb=jnp.broadcast_to(gp,(CH,128))
            rr=rrow_ref[pl.ds(k,1),:]
            rb=jnp.concatenate([jnp.broadcast_to(rr[:,m*128:(m+1)*128],(128,128)).T for m in range(CH//128)],axis=0)
            dq=gpb*y
            hib=(rb>>7).astype(f32).astype(bf)
            hot=jnp.where((rb&127)==lane,gpb,0.0).astype(bf)
            per=CH//NJ
            for j in range(NJ):
                r=rp_ref[j*JB:(j+1)*JB,:]
                s=dg(qh,r,1,1)
                sb=s.astype(bf)
                gn=[];g2=[]
                for h in range(JB//128):
                    jj=j*(JB//128)+h
                    th=jnp.tanh(sb[:,h*128:(h+1)*128])
                    wj=w[jj:jj+1,:]
                    g=th*wj+wj
                    gn.append(g)
                    g2.append(g+jnp.where(hib==bf(jj),hot,bf(0)))
                gn=jnp.concatenate(gn,axis=1);g2=jnp.concatenate(g2,axis=1)
                dq=dq+dg(gn,r,1,0)
                drt[:,j*JB:(j+1)*JB]+=dg(qt,g2,1,0)
                gather(gbase,other,j*per,per)
                scatter(sbase,other,j*per,per)
            dqb=dq.astype(bf)
            dxs[slot][...]=dg(dqb,op,1,1)
            op_out[pl.ds(rel,1)]+=dg(xb,dqb,0,0)[None]
        return 0
    lax.fori_loop(0,count,batch,0)
    outgoing=pltpu.make_async_copy(op_out,op_any,out_sem.at[0])
    outgoing.start()
    scatter(count-1,0,0,CH)
    @pl.loop(0,E//128)
    def _(t):
        sl=pl.ds(pl.multiple_of(t*128,128),128)
        tot=accs[0][sl,:]
        for a in accs[1:]: tot=tot+a[sl,:]
        left_out[sl,:]=tot
        right_out[sl,:]=drt[:,sl].T.astype(right_out.dtype)
    outgoing.wait()
def train(count,rels,lids,rids,negs,entities,right_bf,relations):
    E=entities.shape[0]; NBAT,B=lids.shape; R=relations.shape[0]
    V=pltpu.VMEM; S=pltpu.SMEM
    sp=lambda m: pl.BlockSpec(memory_space=m)
    def body(*refs):
        ins=refs[:22]; ops,x0,y0,d0,rpf,drt,sems=refs[22:29]
        train_kernel(*ins,ops,(x0,),(y0,),(d0,),rpf,drt,sems,*refs[29:])
    D=pltpu.SemaphoreType.DMA
    ids=(NBAT,B)
    return pl.pallas_call(body,name="train",
      in_specs=[sp(S),sp(S)]+[sp(pl.ANY)]*7,
      out_specs=[sp(V),sp(V),sp(pl.ANY)],
      out_shape=[jax.ShapeDtypeStruct((E,128),f32),jax.ShapeDtypeStruct((E,128),bf),jax.ShapeDtypeStruct((R,128,128),f32)],
      scratch_shapes=[S((NBAT*B,),jnp.int32),S((NBAT*B,),jnp.int32),V((E,128),f32),V((E,128),bf),V(ids,jnp.int32),V(ids,jnp.int32),V((R,128,128),f32),D((6,)),D((1,)),D((2,NBAT))]
        +[V((NBAT,128,128),f32)]+[V((CH,128),f32)]*3+[V((E,128),f32),V((128,E),f32),D((NBAT,))]+[V((E,128),f32)]*ACC,
      compiler_params=pltpu.CompilerParams(vmem_limit_bytes=58<<20),
    )(count,rels,lids,rids,entities,right_bf,rids,negs,relations)


MESH = pl.DeviceIdType.MESH
GROUPS = ((0, 48, "zyx"), (48, 48, "yxz"), (96, 32, "xzy"))


def op_sum_kernel(g_ref, e_ref, out, e_out, own, sib, snd, r1a, r1b, r1c, t1a, t1b, t1c, r2a, r2b, r2c, t2a, t2b, t2c, r3a, r3b, r3c,
                  local_sem, a_sem, s1_sem, s2_sem, s3_sem, g1_sem, g2_sem, g3_sem, c_sem, e_sem):
    r1s, t1s, r2s, t2s, r3s = (r1a, r1b, r1c), (t1a, t1b, t1c), (r2a, r2b, r2c), (t2a, t2b, t2c), (r3a, r3b, r3c)
    b = lax.axis_index("bucket")
    core = b % 2
    me = {"y": b // 16, "x": (b // 4) % 4, "z": lax.axis_index("grp") * 2 + (b // 2) % 2}

    def device(at, c):
        return {"bucket": at["y"] * 16 + at["x"] * 4 + (at["z"] % 2) * 2 + c, "grp": at["z"] // 2}

    def moved(axis, o):
        return dict(me, **{axis: (me[axis] + o) % 4})

    def peer(axis, o):
        return device(moved(axis, o), core)

    sibling = device(me, 1 - core)

    def send(src, dst, sems, at, target):
        return pltpu.make_async_remote_copy(src_ref=src, dst_ref=dst, send_sem=sems.at[(0,) + at], recv_sem=sems.at[(1,) + at],
                                            device_id=target, device_id_type=MESH)

    barrier = pltpu.get_barrier_semaphore()
    pl.semaphore_signal(barrier, inc=1, device_id=sibling, device_id_type=MESH)
    for axis in "yxz":
        for o in (1, 2, 3):
            pl.semaphore_signal(barrier, inc=1, device_id=peer(axis, o), device_id_type=MESH)
    locals_ = []
    order = [(me["y"] + o) % 4 for o in (1, 2, 3, 0)]
    for i, p in enumerate(order):
        c = pltpu.make_async_copy(g_ref.at[core, p], own.at[p], local_sem.at[i])
        c.start()
        locals_.append(c)
    pl.semaphore_wait(barrier, 10)
    exchange = send(e_ref, e_out, e_sem, (0,), peer("z", 2))
    exchange.start()
    across = []
    for i, p in enumerate(order):
        c = send(g_ref.at[1 - core, p], sib.at[p], a_sem, (i,), sibling)
        c.start()
        across.append(c)
    firsts = []
    for i, p in enumerate(order):
        locals_[i].wait()
        across[i].wait_recv()

        @pl.loop(0, 4)
        def _(x):
            total = own[p, x] + sib[p, x]
            own[p, x] = total
            snd[p, x] = total.astype(bf)

        for o in (1, 2, 3):
            rows = pl.ds(0, 48)
            c = send(snd.at[p, :, (me["z"] + o) % 4, rows], r1a.at[o - 1, p], s1_sem, (0, o - 1, i), peer("z", o))
            c.start()
            firsts.append((0, c))
            rows = pl.ds(96, 32)
            c = send(snd.at[p, (me["x"] + o) % 4, :, rows], r1c.at[o - 1, :, p], s1_sem, (2, o - 1, i), peer("x", o))
            c.start()
            firsts.append((2, c))
        if i < 3:
            o = i + 1
            c = send(snd.at[p, :, :, pl.ds(48, 48)], r1b.at[o - 1], s1_sem, (1, o - 1, 0), peer("y", o))
            c.start()
            firsts.append((1, c))
    seconds, thirds, gathers = [], [], {}
    for k, (start, n, axes) in enumerate(GROUPS):
        rows = pl.ds(start, n)
        for g, c in firsts:
            if g == k:
                c.wait_recv()

        @pl.loop(0, 4)
        def _(u):
            for v in range(4):
                part = (own.at[u, v, me["z"], rows], own.at[me["y"], u, v, rows], own.at[v, me["x"], u, rows])[k][...]
                for o in range(3):
                    part = part + r1s[k][o, u, v].astype(f32)
                t1s[k][u, v] = part

        for o in (1, 2, 3):
            c = send(t1s[k].at[(me[axes[1]] + o) % 4], r2s[k].at[o - 1], s2_sem, (k, o - 1), peer(axes[1], o))
            c.start()
            seconds.append(c)
    for k, (start, n, axes) in enumerate(GROUPS):
        for c in seconds[3 * k:3 * k + 3]:
            c.wait_recv()
        t2s[k][...] = t1s[k][me[axes[1]]] + r2s[k][0] + r2s[k][1] + r2s[k][2]
        for o in (1, 2, 3):
            c = send(t2s[k].at[(me[axes[2]] + o) % 4], r3s[k].at[o - 1], s3_sem, (k, o - 1), peer(axes[2], o))
            c.start()
            thirds.append(c)

    def place(k, free, at):
        start, n, _ = GROUPS[k]
        index = tuple(slice(None) if a in free else at[a] for a in "yxz")
        return out.at[(core,) + index + (pl.ds(start, n),)]

    def spread(k, level, sems):
        axes = GROUPS[k][2]
        ref = place(k, axes[level + 1:], me)
        gathers[level, k] = [send(ref, ref, sems, (k, o - 1), peer(axes[level], o)) for o in (1, 2, 3)]
        for c in gathers[level, k]:
            c.start()

    for k, (start, n, axes) in enumerate(GROUPS):
        for c in thirds[3 * k:3 * k + 3]:
            c.wait_recv()
        total = t2s[k][me[axes[2]]] + r3s[k][0] + r3s[k][1] + r3s[k][2]
        out[core, me["y"], me["x"], me["z"], pl.ds(start, n)] = total.astype(bf)
        spread(k, 2, g1_sem)
    for k in range(3):
        for c in gathers[2, k]:
            c.wait_recv()
        spread(k, 1, g2_sem)
    kept = []

    def keep(k, ref, i):
        c = send(ref, ref, c_sem, (k, i), sibling)
        c.start()
        kept.append(c)

    for k in range(3):
        for c in gathers[1, k]:
            c.wait_recv()
        spread(k, 0, g3_sem)
        keep(k, place(k, GROUPS[k][2][1:], me), 3)
    for k in range(3):
        axes = GROUPS[k][2]
        for o in (1, 3, 2):
            gathers[0, k][o - 1].wait_recv()
            keep(k, place(k, axes[1:], moved(axes[0], 4 - o)), o - 1)
    for c in kept:
        c.wait_recv()
    for c in across + [c for _, c in firsts] + seconds + thirds + sum(gathers.values(), []) + kept:
        c.wait_send()
    exchange.wait()


def op_total(op_sum, rows):
    V = pltpu.VMEM
    D = pltpu.SemaphoreType.DMA
    ns = [n for _, n, _ in GROUPS]
    shapes = [V((4, 4, 4, 128, 128), f32), V((4, 4, 4, 128, 128), f32), V((4, 4, 4, 128, 128), bf)]
    shapes += [V((3, 4, 4, n, 128), bf) for n in ns] + [V((4, 4, n, 128), f32) for n in ns]
    shapes += [V((3, 4, n, 128), f32) for n in ns] + [V((4, n, 128), f32) for n in ns] + [V((3, n, 128), f32) for n in ns]
    sems = [D((4,)), D((2, 4)), D((2, 3, 3, 4))] + [D((2, 3, 3))] * 5 + [D((2, 3, 4)), D((2, 1))]
    out, other = pl.pallas_call(
        op_sum_kernel,
        name="op_total",
        in_specs=[pl.BlockSpec(memory_space=pl.ANY), pl.BlockSpec(memory_space=V)],
        out_specs=[pl.BlockSpec(memory_space=V)] * 2,
        out_shape=[jax.ShapeDtypeStruct((2, 4, 4, 4, 128, 128), bf), jax.ShapeDtypeStruct(rows.shape, bf)],
        scratch_shapes=shapes + sems,
        compiler_params=pltpu.CompilerParams(collective_id=0, has_side_effects=True, vmem_limit_bytes=58 << 20),
    )(op_sum.reshape(2, 4, 4, 4, 128, 128), rows)
    return out.reshape(128, 128, 128), other


def op_update_kernel(g_ref, p_ref, a_ref, np_ref, na_ref):
    g = g_ref[...].astype(f32)
    acc = a_ref[...] + jnp.mean(g * g, axis=-1)
    na_ref[...] = acc
    np_ref[...] = p_ref[...] - g * (0.1 / jnp.sqrt(acc))[..., None]


def op_update(total, relations, rel_accum):
    n = 32
    cube = pl.BlockSpec((n, 128, 128), lambda i: (i, 0, 0))
    rows = pl.BlockSpec((n, 128), lambda i: (i, 0))
    return pl.pallas_call(op_update_kernel, name="op_update", grid=(128 // n,), in_specs=[cube, cube, rows], out_specs=[cube, rows],
                          out_shape=[jax.ShapeDtypeStruct(relations.shape, f32), jax.ShapeDtypeStruct(rel_accum.shape, f32)],
                          compiler_params=pltpu.CompilerParams(vmem_limit_bytes=58 << 20))(total, relations, rel_accum)


def adagrad_rows(param, accum, grad):
    new_accum = accum + jnp.mean(grad * grad, axis=-1)
    return (param - RATE * grad / jnp.sqrt(new_accum)[..., None], new_accum)


def shifted(value, steps):
    count = lax.axis_size("bucket")

    def one(d):
        return lambda v: lax.ppermute(v, "bucket", [(s, (s + d) % count) for s in range(count)])

    return lax.switch(steps - 1, [one(d) for d in range(1, count)], value)


def local(entities, ent_accum, relations, rel_accum, left_index, right_index, batch_rel, neg_index, batch_count, shift):
    bucket_size = lax.axis_size("bucket")
    backward = 1 + shift[0] % (bucket_size - 1)
    right_part = shifted(entities.astype(bf), bucket_size - backward)
    left_sum, right_sum, op_sum = train(batch_count[0], batch_rel[0, 0], left_index[0, 0], right_index[0, 0], neg_index[0, 0], entities, right_part, relations)
    own = (left_sum + shifted(right_sum, backward).astype(f32)).astype(bf)
    operator_total, other = op_total(op_sum, own)
    new_relations, new_rel_accum = op_update(operator_total, relations, rel_accum)
    new_entities, new_ent_accum = adagrad_rows(entities, ent_accum, own.astype(f32) + other.astype(f32))
    return (new_entities, new_ent_accum, new_relations, new_rel_accum)


def solution(mesh):
    placed = (
        P("bucket", None),
        P("bucket"),
        P(),
        P(),
        P("bucket", "grp", None, None),
        P("bucket", "grp", None, None),
        P("bucket", "grp", None),
        P("bucket", "grp", None, None),
        P("bucket", "grp"),
        P(),
    )
    return jax.shard_map(
        local,
        mesh=mesh,
        in_specs=placed,
        out_specs=(P("bucket", None), P("bucket"), P(), P()),
        check_vma=False,
    )
```
